512 devices in a mesh: row: 16 (over y, x), col: 32 (over z, core).
Axes of the slice: x: 4, y: 4, z: 16, core: 2. Of those that a mesh axis runs over, the one named last changes fastest.
Arguments:
- momentum: float32 [4608, 8192], P('row', 'col'), may hold values from -37 to 37
Outputs:
- update: float32 [4608, 8192], P('row', 'col')
The draws below stay inside these ranges and needn't reach their ends.
All inputs are finite; a program needn't handle non-finite values.
Results may differ from the reference program's by a relative error of at most 0.0049.
Values may be sent and summed in bfloat16 or wider, within the bound.
A program may use at most 64 MiB of HBM per device.

```python
import math
import jax
import jax.numpy as jnp

ROWS = 4608
COLS = 8192


def draw_momentum(key, part):
    keys = jax.random.split(key, 3)
    row_pos = jnp.arange(ROWS, dtype=jnp.float32) / ROWS
    col_pos = jnp.arange(COLS, dtype=jnp.float32) / COLS
    ramp_rate = 0.5 * math.log(3.0)
    row_scale = jnp.exp(ramp_rate * row_pos + 0.35 * jax.random.uniform(keys[1], (ROWS,), jnp.float32))
    col_scale = jnp.exp(ramp_rate * col_pos + 0.35 * jax.random.uniform(keys[2], (COLS,), jnp.float32))
    base = jnp.clip(jax.random.normal(keys[0], (ROWS, COLS), jnp.float32), -6.0, 6.0)
    return base * row_scale[:, None] * col_scale[None, :]


def setup_inputs(seed: int = 0) -> dict:
    seeds = jax.random.split(jax.random.key(seed), 2)
    momentum = draw_momentum(jax.random.fold_in(seeds[1], 71), 0)
    return {"momentum": momentum}


quintic_a = 3.4445
quintic_b = -4.775
quintic_c = 2.0315

def reference(momentum):
    norm_squares = jnp.sum(momentum * momentum)
    factor = 0.6 * math.sqrt(ROWS) / (jnp.sqrt(norm_squares) + 1e-07)
    scaled = (momentum * factor).astype(jnp.bfloat16)
    gram = jnp.dot(scaled, scaled.T, preferred_element_type=jnp.float32).astype(jnp.bfloat16)
    squared = jnp.dot(gram, gram, preferred_element_type=jnp.float32)
    poly = (quintic_b * gram.astype(jnp.float32) + quintic_c * squared).astype(jnp.bfloat16)
    product = jnp.dot(poly, scaled, preferred_element_type=jnp.float32)
    return math.sqrt(COLS) * (quintic_a * scaled.astype(jnp.float32) + product)
```

```python
import functools
import math

import jax
import jax.numpy as jnp
from jax import lax
from jax.experimental import pallas as pl
from jax.experimental.pallas import tpu as pltpu
from jax.sharding import PartitionSpec as P

ROWS = 4608
COLS = 8192

quintic_a = 3.4445
quintic_b = -4.775
quintic_c = 2.0315

MESH = pl.DeviceIdType.MESH
F32 = jnp.float32
BF16 = jnp.bfloat16

BLOCK = 288
WIDTH = 256
PANEL = 4 * BLOCK
HALF = PANEL // 2
GROUP = 384
GROUPS = PANEL // GROUP
CHUNK = 112
STACK = 16 * CHUNK
PARTS = ((0, 64), (64, 48))
NP = len(PARTS)
STEP4 = (1, 3, 2)


def rows_product(left, right):
    return lax.dot_general(left, right, (((1,), (1,)), ((), ())), preferred_element_type=F32)


def columns_product(left, right):
    return lax.dot_general(left, right, (((0,), (0,)), ((), ())), preferred_element_type=F32)


def kernel(
    m_ref,
    out_ref,
    row_f, col_f, row_o, col_o,
    row_b, col_b, row_ob, col_ob,
    part, gram, ring_p, ring_m,
    tiles, tile_in,
    w, wb, wb2, y_all, y_in, z_in, y_own,
    tile_s, tile_r, bulk_s, bulk_r, pass_s, pass_r,
    rs_s, rs_r, ag_s, ag_r, swap_s, swap_r,
    ys_s, ys_r, yg_s, yg_r, zs_s, zs_r,
):
    row, col = lax.axis_index("row"), lax.axis_index("col")
    y, x, z, k = row // 4, row % 4, col // 2, col % 2

    def at_x(d):
        return (y * 4 + (x + d) % 4, col)

    def at_y(d):
        return (((y + d) % 4) * 4 + x, col)

    def at_z(d):
        return (row, ((z + d) % 16) * 2 + k)

    other = (row, z * 2 + 1 - k)

    def send(src, dst, ss, rs, device):
        return pltpu.make_async_remote_copy(
            src_ref=src, dst_ref=dst, send_sem=ss, recv_sem=rs, device_id=device, device_id_type=MESH
        )

    sent = []

    barrier = pltpu.get_barrier_semaphore()
    peers = [at_x(d) for d in STEP4] + [at_y(d) for d in STEP4] + [other]
    peers += [at_z(d) for d in (1, 15, 2, 14, 4, 12)]
    for peer in peers:
        pl.semaphore_signal(barrier, inc=1, device_id=peer, device_id_type=MESH)

    squares = m_ref[...] * m_ref[...]
    squares = jnp.sum(squares.reshape(BLOCK // 8, 8, WIDTH), axis=0)
    tiles[0] = squares[:, :128] + squares[:, 128:]
    part[STACK - 64 : STACK, :] = jnp.zeros((64, GROUP), F32)

    pl.semaphore_wait(barrier, len(peers))

    def tile_copy(stage, slot, device, src=None):
        src = tiles.at[stage] if src is None else src
        return send(src, tile_in.at[slot], tile_s.at[slot], tile_r.at[slot], device)

    def exchange(stage, slots):
        for slot, device in slots:
            c = tile_copy(stage, slot, device)
            c.start()
            sent.append(c)

    def block(ref, t, rows=BLOCK):
        return ref.at[pl.ds(pl.multiple_of(t * rows, 16), rows), :]

    z1 = [(0, at_z(1)), (1, at_z(15)), (2, at_z(2))]
    exchange(0, z1)
    bulk = []
    for i, d in enumerate(STEP4):
        for j, (dst, here, device) in enumerate(((row_f, x, at_x(d)), (col_f, y, at_y(d)))):
            c = send(m_ref, block(dst, here), bulk_s.at[j, i], bulk_r.at[j, i], device)
            c.start()
            sent.append(c)
            bulk.append(c)

    def pass_rows(src, t):
        c = send(src, block(row_o, t % 2), pass_s.at[0, t % 2], pass_r.at[0, t % 2], other)

        @pl.when(t // 2 != k)
        def _():
            c.start()

    def pass_cols(src, t):
        c = send(src, block(col_o, t), pass_s.at[1, t], pass_r.at[1, t], other)
        c.start()

    pass_rows(m_ref, x)
    pass_cols(m_ref, y)

    def gather_tiles(slots):
        for slot, device in slots:
            tile_copy(0, slot, device).wait_recv()

    gather_tiles(z1)
    tiles[1] = tiles[0] + tile_in[0] + tile_in[1] + tile_in[2]
    z2 = [(3, at_z(4)), (4, at_z(12))]
    exchange(1, z2)
    gather_tiles(z2[:1])
    c = tile_copy(1, 5, at_z(4), tile_in.at[3])
    c.start()
    sent.append(c)
    gather_tiles(z2[1:])
    c.wait_recv()
    tiles[2] = tiles[1] + tile_in[3] + tile_in[4] + tile_in[5]
    x1 = [(6 + i, at_x(d)) for i, d in enumerate(STEP4)]
    exchange(2, x1)

    for i, d in enumerate(STEP4):
        bulk[2 * i].wait_recv()
        pass_rows(block(row_f, (x + 4 - d) % 4), (x + 4 - d) % 4)
        bulk[2 * i + 1].wait_recv()
        pass_cols(block(col_f, (y + 4 - d) % 4), (y + 4 - d) % 4)

    gather_tiles(x1)
    tiles[3] = tiles[2] + tile_in[6] + tile_in[7] + tile_in[8]
    y1 = [(9 + i, at_y(d)) for i, d in enumerate(STEP4)]
    exchange(3, y1)
    gather_tiles(y1)
    tiles[4] = tiles[3] + tile_in[9] + tile_in[10] + tile_in[11]
    k1 = [(12, other)]
    exchange(4, k1)
    gather_tiles(k1)
    norm_squares = jnp.sum(tiles[4] + tile_in[12])
    factor = 0.6 * math.sqrt(ROWS) / (jnp.sqrt(jnp.full((8, 128), norm_squares, F32)) + 1e-07)
    factor = factor[0:1, 0:1]

    block(row_f, x)[...] = m_ref[...]
    block(col_f, y)[...] = m_ref[...]

    def scale(t, carry):
        at = pl.ds(pl.multiple_of(t * BLOCK, 16), BLOCK)
        row_b[at, :] = (row_f[at, :] * factor).astype(BF16)
        col_b[at, :] = (col_f[at, :] * factor).astype(BF16)
        return carry

    lax.fori_loop(0, 4, scale, 0)

    for t in range(2):
        send(m_ref, block(row_o, t), pass_s.at[0, t], pass_r.at[0, t], other).wait_recv()
    for t in range(4):
        send(m_ref, block(col_o, t), pass_s.at[1, t], pass_r.at[1, t], other).wait_recv()

    def scale_other(t, carry):
        at = pl.ds(pl.multiple_of(t * BLOCK, 16), BLOCK)
        col_ob[at, :] = (col_o[at, :] * factor).astype(BF16)
        return carry

    lax.fori_loop(0, 4, scale_other, 0)

    def scale_rows(t, carry):
        at = pl.ds(pl.multiple_of(t * BLOCK, 16), BLOCK)
        row_ob[at, :] = (row_o[at, :] * factor).astype(BF16)
        return carry

    lax.fori_loop(0, 2, scale_rows, 0)

    mine = pl.ds(pl.multiple_of(k * HALF, HALF), HALF)

    def gram_group(n, carry):
        at = pl.ds(pl.multiple_of(n * GROUP, GROUP), GROUP)
        total = rows_product(row_b[mine, :], col_b[at, :])
        total += rows_product(row_ob[...], col_ob[at, :])
        part[pl.ds(pl.multiple_of(n * HALF, HALF), HALF), :] = total
        return carry

    lax.fori_loop(0, GROUPS, gram_group, 0)

    def piece(c, p):
        return pl.ds(pl.multiple_of((c + 32) % 16 * CHUNK + PARTS[p][0], 16), PARTS[p][1])

    def inside(p):
        return pl.ds(PARTS[p][0], PARTS[p][1])

    def hop(d, s, p):
        ring = (ring_p, ring_m)[d]
        return send(
            ring.at[s, inside(p)], ring.at[s + 1, inside(p)],
            rs_s.at[d, s, p], rs_r.at[d, s, p], (at_z(1), at_z(15))[d],
        )

    for p in range(NP):
        ring_p[0, inside(p)] = part[piece(z + 8, p), :].astype(BF16)
        hop(0, 0, p).start()
        ring_m[0, inside(p)] = part[piece(z - 7, p), :].astype(BF16)
        hop(1, 0, p).start()

    def plus_step(s, p):
        hop(0, s - 1, p).wait_recv()
        ring_p[s, inside(p)] = (ring_p[s, inside(p)].astype(F32) + part[piece(z + 8 - s, p), :]).astype(BF16)
        hop(0, s, p).start()

    def minus_step(s, p):
        hop(1, s - 1, p).wait_recv()
        ring_m[s, inside(p)] = (ring_m[s, inside(p)].astype(F32) + part[piece(z - 7 + s, p), :]).astype(BF16)
        hop(1, s, p).start()

    def reduce_step(s, carry):
        for p in range(NP):
            plus_step(s, p)
            minus_step(s, p)
        return carry

    lax.fori_loop(1, 7, reduce_step, 0)
    for p in range(NP):
        plus_step(7, p)

    def onward(d, s, p):
        c = (z - s, z + s)[d]
        at = gram.at[k, piece(c, p)]
        return send(at, at, ag_s.at[d, s, p], ag_r.at[d, s, p], (at_z(1), at_z(15))[d])

    def arrived(d, s, p):
        c = (z - 1 - s, z + 1 + s)[d]
        at = gram.at[k, piece(c, p)]
        send(at, at, ag_s.at[d, s, p], ag_r.at[d, s, p], (at_z(1), at_z(15))[d]).wait_recv()

    def swap(slot, c, p):
        at = gram.at[k, piece(c, p)]
        return send(at, at, swap_s.at[slot, p], swap_r.at[slot, p], other)

    for p in range(NP):
        hop(0, 7, p).wait_recv()
        hop(1, 6, p).wait_recv()
        total = part[piece(z, p), :] + ring_p[8, inside(p)].astype(F32) + ring_m[7, inside(p)].astype(F32)
        gram[k, piece(z, p), :] = total.astype(BF16)
        onward(0, 0, p).start()
        onward(1, 0, p).start()
        swap(0, z, p).start()

    def gather_step(s, carry):
        for p in range(NP):
            arrived(0, s - 1, p)
            onward(0, s, p).start()
            swap(s, z - s, p).start()
            arrived(1, s - 1, p)
            onward(1, s, p).start()
            swap(8 + s, z + s, p).start()
        return carry

    lax.fori_loop(1, 7, gather_step, 0)
    for p in range(NP):
        arrived(0, 6, p)
        onward(0, 7, p).start()
        swap(7, z - 7, p).start()
        arrived(1, 6, p)
        swap(15, z + 7, p).start()
    for p in range(NP):
        arrived(0, 7, p)
        swap(8, z - 8, p).start()

    def swapped(s, carry):
        for p in range(NP):
            at = gram.at[1 - k, inside(p)]
            send(at, at, swap_s.at[s, p], swap_r.at[s, p], other).wait_recv()
        return carry

    lax.fori_loop(0, 16, swapped, 0)

    def times_gram(panel_0, panel_1, keep):
        @pl.when(k == 0)
        def _():
            def half(h, carry):
                total = jnp.zeros((HALF, WIDTH), F32)
                for n in range(GROUPS):
                    total += jnp.dot(
                        gram[h, n * HALF : (n + 1) * HALF, :],
                        panel_0[n * GROUP : (n + 1) * GROUP, :],
                        preferred_element_type=F32,
                    )
                at = pl.ds(pl.multiple_of(h * HALF, HALF), HALF)
                w[at, :] = total
                keep[at, :] = total.astype(BF16)
                return carry

            lax.fori_loop(0, 2, half, 0)

        @pl.when(k == 1)
        def _():
            def group(n, carry):
                total = jnp.zeros((GROUP, WIDTH), F32)
                for h in range(2):
                    total += columns_product(
                        gram[h, pl.ds(pl.multiple_of(n * HALF, HALF), HALF), :],
                        panel_1[h * HALF : (h + 1) * HALF, :],
                    )
                at = pl.ds(pl.multiple_of(n * GROUP, GROUP), GROUP)
                w[at, :] = total
                keep[at, :] = total.astype(BF16)
                return carry

            lax.fori_loop(0, GROUPS, group, 0)

    first = k == 0
    o_sum, o_all = jnp.where(first, x, y), jnp.where(first, y, x)

    def ring_sum(d):
        t = (o_sum + d) % 4
        return t, (jnp.where(first, y * 4 + t, t * 4 + x), col)

    def ring_all(d):
        t = (o_all + d) % 4
        return (jnp.where(first, t * 4 + x, y * 4 + t), col)

    def scatter(src, dst, ss, rs):
        copies = []
        for i, d in enumerate(STEP4):
            t, device = ring_sum(d)
            c = send(block(src, t), dst.at[i], ss.at[i], rs.at[i], device)
            c.start()
            sent.append(c)
            copies.append(c)
        total = block(w, o_sum)[...]
        for i, c in enumerate(copies):
            c.wait_recv()
            total += dst[i].astype(F32)
        return total

    times_gram(col_b, row_b, wb)
    y_own[...] = scatter(wb, y_in, ys_s, ys_r)
    block(y_all, o_all)[...] = y_own[...].astype(BF16)
    copies = []
    for i, d in enumerate(STEP4):
        c = send(block(y_all, o_all), block(y_all, o_all), yg_s.at[i], yg_r.at[i], ring_all(d))
        c.start()
        sent.append(c)
        copies.append(c)
    for c in copies:
        c.wait_recv()
    times_gram(y_all, y_all, wb2)
    z_own = scatter(wb2, z_in, zs_s, zs_r)
    scaled = block(row_b, x)[...].astype(F32)
    out_ref[...] = math.sqrt(COLS) * (quintic_a * scaled + (quintic_b * y_own[...] + quintic_c * z_own))

    for c in sent:
        c.wait_send()
    for t in range(2):
        send(block(row_o, t), block(row_o, t), pass_s.at[0, t], pass_r.at[0, t], other).wait_send()
    for t in range(4):
        send(block(col_o, t), block(col_o, t), pass_s.at[1, t], pass_r.at[1, t], other).wait_send()

    def left(s, carry):
        for p in range(NP):
            hop(0, s, p).wait_send()
            hop(1, s, p).wait_send()
            onward(0, s, p).wait_send()
            onward(1, s, p).wait_send()
            swap(s, z, p).wait_send()
            swap(8 + s, z, p).wait_send()
        return carry

    lax.fori_loop(0, 7, left, 0)
    for p in range(NP):
        hop(0, 7, p).wait_send()
        onward(0, 7, p).wait_send()
        swap(7, z, p).wait_send()
        swap(15, z, p).wait_send()


def body(momentum):
    dma = pltpu.SemaphoreType.DMA
    return pl.pallas_call(
        kernel,
        out_shape=jax.ShapeDtypeStruct((BLOCK, WIDTH), F32),
        in_specs=[pl.BlockSpec(memory_space=pltpu.VMEM)],
        out_specs=pl.BlockSpec(memory_space=pltpu.VMEM),
        scratch_shapes=[
            pltpu.VMEM((PANEL, WIDTH), F32),
            pltpu.VMEM((PANEL, WIDTH), F32),
            pltpu.VMEM((HALF, WIDTH), F32),
            pltpu.VMEM((PANEL, WIDTH), F32),
            pltpu.VMEM((PANEL, WIDTH), BF16),
            pltpu.VMEM((PANEL, WIDTH), BF16),
            pltpu.VMEM((HALF, WIDTH), BF16),
            pltpu.VMEM((PANEL, WIDTH), BF16),
            pltpu.VMEM((STACK, GROUP), F32),
            pltpu.VMEM((2, STACK, GROUP), BF16),
            pltpu.VMEM((9, CHUNK, GROUP), BF16),
            pltpu.VMEM((8, CHUNK, GROUP), BF16),
            pltpu.VMEM((5, 8, 128), F32),
            pltpu.VMEM((13, 8, 128), F32),
            pltpu.VMEM((PANEL, WIDTH), F32),
            pltpu.VMEM((PANEL, WIDTH), BF16),
            pltpu.VMEM((PANEL, WIDTH), BF16),
            pltpu.VMEM((PANEL, WIDTH), BF16),
            pltpu.VMEM((3, BLOCK, WIDTH), BF16),
            pltpu.VMEM((3, BLOCK, WIDTH), BF16),
            pltpu.VMEM((BLOCK, WIDTH), F32),
            dma((13,)), dma((13,)),
            dma((2, 3)), dma((2, 3)),
            dma((2, 4)), dma((2, 4)),
            dma((2, 8, NP)), dma((2, 8, NP)),
            dma((2, 8, NP)), dma((2, 8, NP)),
            dma((16, NP)), dma((16, NP)),
            dma((3,)), dma((3,)), dma((3,)), dma((3,)), dma((3,)), dma((3,)),
        ],
        compiler_params=pltpu.CompilerParams(
            collective_id=0, has_side_effects=True, vmem_limit_bytes=48 * 2**20
        ),
        name="muon",
    )(momentum)


def solution(mesh):
    return jax.shard_map(
        body, mesh=mesh, in_specs=(P("row", "col"),), out_specs=P("row", "col"), check_vma=False
    )
```

```python
import functools
import math

import jax
import jax.numpy as jnp
from jax import lax
from jax.experimental import pallas as pl
from jax.experimental.pallas import tpu as pltpu
from jax.sharding import PartitionSpec as P

ROWS = 4608
COLS = 8192

quintic_a = 3.4445
quintic_b = -4.775
quintic_c = 2.0315

MESH = pl.DeviceIdType.MESH
F32 = jnp.float32
BF16 = jnp.bfloat16

BLOCK = 288
WIDTH = 256
PANEL = 4 * BLOCK
HALF = PANEL // 2
GROUP = 384
GROUPS = PANEL // GROUP
CHUNK = 112
STACK = 16 * CHUNK
PARTS = ((0, 64), (64, 48))
NP = len(PARTS)
STEP4 = (1, 3, 2)


def rows_product(left, right):
    return lax.dot_general(left, right, (((1,), (1,)), ((), ())), preferred_element_type=F32)


def columns_product(left, right):
    return lax.dot_general(left, right, (((0,), (0,)), ((), ())), preferred_element_type=F32)


def kernel(
    m_hbm,
    out_ref,
    m_ref, m_b, row_b, col_b, row_ob, col_ob, x_f, x_b,
    part, gram, ring_p, ring_m,
    tiles, tile_in,
    w, wb, wb2, y_all, y_in, z_in, y_own,
    load_s, tile_s, tile_r, bulk_s, bulk_r, pass_s, pass_r, wide_s, wide_r,
    rs_s, rs_r, ag_s, ag_r, swap_s, swap_r,
    ys_s, ys_r, yg_s, yg_r, zs_s, zs_r,
):
    row, col = lax.axis_index("row"), lax.axis_index("col")
    y, x, z, k = row // 4, row % 4, col // 2, col % 2
    first = k == 0

    def at_x(d):
        return (y * 4 + (x + d) % 4, col)

    def at_y(d):
        return (((y + d) % 4) * 4 + x, col)

    def at_z(d):
        return (row, ((z + d) % 16) * 2 + k)

    other = (row, z * 2 + 1 - k)

    o_sum, o_all = jnp.where(first, x, y), jnp.where(first, y, x)

    def ring_sum(d):
        t = (o_sum + d) % 4
        return t, (jnp.where(first, y * 4 + t, t * 4 + x), col)

    def ring_all(d):
        t = (o_all + d) % 4
        return (jnp.where(first, t * 4 + x, y * 4 + t), col)

    def send(src, dst, ss, rs, device):
        return pltpu.make_async_remote_copy(
            src_ref=src, dst_ref=dst, send_sem=ss, recv_sem=rs, device_id=device, device_id_type=MESH
        )

    sent = []

    def start(src, dst, ss, rs, device):
        c = send(src, dst, ss, rs, device)
        c.start()
        sent.append(c)
        return c

    load = pltpu.make_async_copy(m_hbm, m_ref, load_s)
    load.start()
    barrier = pltpu.get_barrier_semaphore()
    peers = [at_x(d) for d in STEP4] + [at_y(d) for d in STEP4] + [other]
    peers += [at_z(d) for d in (1, 15, 2, 14)]
    for peer in peers:
        pl.semaphore_signal(barrier, inc=1, device_id=peer, device_id_type=MESH)
    load.wait()

    def block(ref, t, rows=BLOCK):
        return ref.at[pl.ds(pl.multiple_of(t * rows, 16), rows), :]

    m_b[...] = m_ref[...].astype(BF16)
    squares = m_ref[...] * m_ref[...]
    squares = jnp.sum(squares.reshape(BLOCK // 8, 8, WIDTH), axis=0)
    tiles[0] = squares[:, :128] + squares[:, 128:]

    pl.semaphore_wait(barrier, len(peers))

    bulk = []
    for i, d in enumerate(STEP4):
        bulk.append(start(m_b, block(row_b, x), bulk_s.at[0, i], bulk_r.at[0, i], at_x(d)))
        bulk.append(start(m_b, block(col_b, y), bulk_s.at[1, i], bulk_r.at[1, i], at_y(d)))

    def pass_rows(src, t):
        @pl.when(t // 2 != k)
        def _():
            send(src, block(row_ob, t % 2), pass_s.at[0, t % 2], pass_r.at[0, t % 2], other).start()

    def pass_cols(src, t):
        send(src, block(col_ob, t), pass_s.at[1, t], pass_r.at[1, t], other).start()

    pass_rows(m_b, x)
    pass_cols(m_b, y)

    def exchange(stage, slots):
        for slot, device in slots:
            start(tiles.at[stage], tile_in.at[slot], tile_s.at[slot], tile_r.at[slot], device)

    def gathered(stage, slots):
        total = tiles[stage]
        for slot, device in slots:
            send(tiles.at[0], tile_in.at[slot], tile_s.at[slot], tile_r.at[slot], device).wait_recv()
            total += tile_in[slot]
        tiles[stage + 1] = total

    near = [(0, at_z(1)), (1, at_z(15)), (2, at_z(2))]
    far = [(3, at_z(4)), (4, at_z(12))]
    along_x = [(6 + i, at_x(d)) for i, d in enumerate(STEP4)]
    along_y = [(9 + i, at_y(d)) for i, d in enumerate(STEP4)]
    exchange(0, near)

    block(row_b, x)[...] = m_b[...]
    block(col_b, y)[...] = m_b[...]
    block(x_f, o_all)[...] = m_ref[...]
    part[STACK - 64 : STACK, :] = jnp.zeros((64, GROUP), F32)

    for i, d in enumerate(STEP4):
        bulk[2 * i].wait_recv()
        pass_rows(block(row_b, (x + 4 - d) % 4), (x + 4 - d) % 4)
        bulk[2 * i + 1].wait_recv()
        pass_cols(block(col_b, (y + 4 - d) % 4), (y + 4 - d) % 4)

    wide = [
        start(m_ref, block(x_f, o_all), wide_s.at[i], wide_r.at[i], ring_all(d)) for i, d in enumerate(STEP4)
    ]

    mine = pl.ds(pl.multiple_of(k * HALF, HALF), HALF)

    def gram_own(n, carry):
        at = pl.ds(pl.multiple_of(n * GROUP, GROUP), GROUP)
        part[pl.ds(pl.multiple_of(n * HALF, HALF), HALF), :] = rows_product(row_b[mine, :], col_b[at, :])
        return carry

    lax.fori_loop(0, GROUPS, gram_own, 0)
    for t in range(2):
        send(m_b, block(row_ob, t), pass_s.at[0, t], pass_r.at[0, t], other).wait_recv()
    for t in range(4):
        send(m_b, block(col_ob, t), pass_s.at[1, t], pass_r.at[1, t], other).wait_recv()

    def gram_other(n, carry):
        at = pl.ds(pl.multiple_of(n * GROUP, GROUP), GROUP)
        part[pl.ds(pl.multiple_of(n * HALF, HALF), HALF), :] += rows_product(row_ob[...], col_ob[at, :])
        return carry

    lax.fori_loop(0, GROUPS, gram_other, 0)

    def piece(c, p):
        return pl.ds(pl.multiple_of((c + 32) % 16 * CHUNK + PARTS[p][0], 16), PARTS[p][1])

    def inside(p):
        return pl.ds(PARTS[p][0], PARTS[p][1])

    def hop(d, s, p):
        ring = (ring_p, ring_m)[d]
        return send(
            ring.at[s, inside(p)], ring.at[s + 1, inside(p)],
            rs_s.at[d, s, p], rs_r.at[d, s, p], (at_z(1), at_z(15))[d],
        )

    for p in range(NP):
        ring_p[0, inside(p)] = part[piece(z + 8, p), :].astype(BF16)
        hop(0, 0, p).start()
        ring_m[0, inside(p)] = part[piece(z - 7, p), :].astype(BF16)
        hop(1, 0, p).start()

    def plus_step(s, p):
        hop(0, s - 1, p).wait_recv()
        ring_p[s, inside(p)] = (ring_p[s, inside(p)].astype(F32) + part[piece(z + 8 - s, p), :]).astype(BF16)
        hop(0, s, p).start()

    def minus_step(s, p):
        hop(1, s - 1, p).wait_recv()
        ring_m[s, inside(p)] = (ring_m[s, inside(p)].astype(F32) + part[piece(z - 7 + s, p), :]).astype(BF16)
        hop(1, s, p).start()

    def reduce_step(s, carry):
        for p in range(NP):
            plus_step(s, p)
            minus_step(s, p)
        return carry

    gathered(0, near)
    lax.fori_loop(1, 4, reduce_step, 0)
    exchange(1, far)
    lax.fori_loop(4, 6, reduce_step, 0)
    send(tiles.at[1], tile_in.at[3], tile_s.at[3], tile_r.at[3], at_z(4)).wait_recv()
    onward_tile = start(tile_in.at[3], tile_in.at[5], tile_s.at[5], tile_r.at[5], at_z(4))
    lax.fori_loop(6, 7, reduce_step, 0)
    for p in range(NP):
        plus_step(7, p)
    send(tiles.at[1], tile_in.at[4], tile_s.at[4], tile_r.at[4], at_z(12)).wait_recv()
    onward_tile.wait_recv()
    tiles[2] = tiles[1] + tile_in[3] + tile_in[4] + tile_in[5]
    exchange(2, along_x)

    def onward(d, s, p):
        at = gram.at[k, piece((z - s, z + s)[d], p)]
        return send(at, at, ag_s.at[d, s, p], ag_r.at[d, s, p], (at_z(1), at_z(15))[d])

    def arrived(d, s, p):
        at = gram.at[k, piece((z - s, z + s)[d], p)]
        send(at, at, ag_s.at[d, s - 1, p], ag_r.at[d, s - 1, p], (at_z(1), at_z(15))[d]).wait_recv()

    def swap(slot, c, p):
        at = gram.at[k, piece(c, p)]
        return send(at, at, swap_s.at[slot, p], swap_r.at[slot, p], other)

    for p in range(NP):
        hop(0, 7, p).wait_recv()
        hop(1, 6, p).wait_recv()
        total = part[piece(z, p), :] + ring_p[8, inside(p)].astype(F32) + ring_m[7, inside(p)].astype(F32)
        gram[k, piece(z, p), :] = total.astype(BF16)
        onward(0, 0, p).start()
        onward(1, 0, p).start()
    for p in range(NP):
        swap(0, z, p).start()

    def gather_step(s, carry):
        for p in range(NP):
            arrived(0, s, p)
            onward(0, s, p).start()
            arrived(1, s, p)
            onward(1, s, p).start()
        for p in range(NP):
            swap(s, z - s, p).start()
            swap(8 + s, z + s, p).start()
        return carry

    lax.fori_loop(1, 3, gather_step, 0)
    gathered(2, along_x)
    exchange(3, along_y)
    lax.fori_loop(3, 5, gather_step, 0)
    gathered(3, along_y)
    exchange(4, [(12, other)])
    lax.fori_loop(5, 6, gather_step, 0)
    gathered(4, [(12, other)])
    norm_squares = jnp.sum(tiles[5])
    factor = 0.6 * math.sqrt(ROWS) / (jnp.sqrt(jnp.full((8, 128), norm_squares, F32)) + 1e-07)
    factor = factor[0:1, 0:1]
    lax.fori_loop(6, 7, gather_step, 0)

    for c in wide:
        c.wait_recv()

    def scale(t, carry):
        at = pl.ds(pl.multiple_of(t * BLOCK, 16), BLOCK)
        x_b[at, :] = (x_f[at, :] * factor).astype(BF16)
        return carry

    lax.fori_loop(0, 4, scale, 0)

    for p in range(NP):
        arrived(0, 7, p)
        onward(0, 7, p).start()
        arrived(1, 7, p)
    for p in range(NP):
        swap(7, z - 7, p).start()
        swap(15, z + 7, p).start()
    for p in range(NP):
        arrived(0, 8, p)
        swap(8, z - 8, p).start()

    def swapped(s, carry):
        for p in range(NP):
            at = gram.at[1 - k, inside(p)]
            send(at, at, swap_s.at[s, p], swap_r.at[s, p], other).wait_recv()
        return carry

    lax.fori_loop(0, 16, swapped, 0)

    squared_factor = factor * factor

    def times_gram(panel, keep):
        @pl.when(first)
        def _():
            def half(h, carry):
                total = jnp.zeros((HALF, WIDTH), F32)
                for n in range(GROUPS):
                    total += jnp.dot(
                        gram[h, n * HALF : (n + 1) * HALF, :],
                        panel[n * GROUP : (n + 1) * GROUP, :],
                        preferred_element_type=F32,
                    )
                at = pl.ds(pl.multiple_of(h * HALF, HALF), HALF)
                total = total * squared_factor
                w[at, :] = total
                keep[at, :] = total.astype(BF16)
                return carry

            lax.fori_loop(0, 2, half, 0)

        @pl.when(k == 1)
        def _():
            def group(n, carry):
                total = jnp.zeros((GROUP, WIDTH), F32)
                for h in range(2):
                    total += columns_product(
                        gram[h, pl.ds(pl.multiple_of(n * HALF, HALF), HALF), :],
                        panel[h * HALF : (h + 1) * HALF, :],
                    )
                at = pl.ds(pl.multiple_of(n * GROUP, GROUP), GROUP)
                total = total * squared_factor
                w[at, :] = total
                keep[at, :] = total.astype(BF16)
                return carry

            lax.fori_loop(0, GROUPS, group, 0)

    def scatter(src, dst, ss, rs):
        copies = []
        for i, d in enumerate(STEP4):
            t, device = ring_sum(d)
            copies.append(start(block(src, t), dst.at[i], ss.at[i], rs.at[i], device))
        total = block(w, o_sum)[...]
        for i, c in enumerate(copies):
            c.wait_recv()
            total += dst[i].astype(F32)
        return total

    times_gram(x_b, wb)
    y_own[...] = scatter(wb, y_in, ys_s, ys_r)
    block(y_all, o_all)[...] = y_own[...].astype(BF16)
    copies = [
        start(block(y_all, o_all), block(y_all, o_all), yg_s.at[i], yg_r.at[i], ring_all(d))
        for i, d in enumerate(STEP4)
    ]
    for c in copies:
        c.wait_recv()
    times_gram(y_all, wb2)
    z_own = scatter(wb2, z_in, zs_s, zs_r)
    scaled = block(x_b, o_all)[...].astype(F32)
    out_ref[...] = math.sqrt(COLS) * (quintic_a * scaled + (quintic_b * y_own[...] + quintic_c * z_own))

    for c in sent:
        c.wait_send()
    for t in range(2):
        send(block(row_ob, t), block(row_ob, t), pass_s.at[0, t], pass_r.at[0, t], other).wait_send()
    for t in range(4):
        send(block(col_ob, t), block(col_ob, t), pass_s.at[1, t], pass_r.at[1, t], other).wait_send()

    def left(s, carry):
        for p in range(NP):
            hop(0, s, p).wait_send()
            hop(1, s, p).wait_send()
            onward(0, s, p).wait_send()
            onward(1, s, p).wait_send()
            swap(s, z, p).wait_send()
            swap(8 + s, z, p).wait_send()
        return carry

    lax.fori_loop(0, 7, left, 0)
    for p in range(NP):
        hop(0, 7, p).wait_send()
        onward(0, 7, p).wait_send()
        swap(7, z, p).wait_send()
        swap(15, z, p).wait_send()


def body(momentum):
    dma = pltpu.SemaphoreType.DMA
    return pl.pallas_call(
        kernel,
        out_shape=jax.ShapeDtypeStruct((BLOCK, WIDTH), F32),
        in_specs=[pl.BlockSpec(memory_space=pltpu.HBM)],
        out_specs=pl.BlockSpec(memory_space=pltpu.VMEM),
        scratch_shapes=[
            pltpu.VMEM((BLOCK, WIDTH), F32),
            pltpu.VMEM((BLOCK, WIDTH), BF16),
            pltpu.VMEM((PANEL, WIDTH), BF16),
            pltpu.VMEM((PANEL, WIDTH), BF16),
            pltpu.VMEM((HALF, WIDTH), BF16),
            pltpu.VMEM((PANEL, WIDTH), BF16),
            pltpu.VMEM((PANEL, WIDTH), F32),
            pltpu.VMEM((PANEL, WIDTH), BF16),
            pltpu.VMEM((STACK, GROUP), F32),
            pltpu.VMEM((2, STACK, GROUP), BF16),
            pltpu.VMEM((9, CHUNK, GROUP), BF16),
            pltpu.VMEM((8, CHUNK, GROUP), BF16),
            pltpu.VMEM((6, 8, 128), F32),
            pltpu.VMEM((13, 8, 128), F32),
            pltpu.VMEM((PANEL, WIDTH), F32),
            pltpu.VMEM((PANEL, WIDTH), BF16),
            pltpu.VMEM((PANEL, WIDTH), BF16),
            pltpu.VMEM((PANEL, WIDTH), BF16),
            pltpu.VMEM((3, BLOCK, WIDTH), BF16),
            pltpu.VMEM((3, BLOCK, WIDTH), BF16),
            pltpu.VMEM((BLOCK, WIDTH), F32),
            dma, dma((13,)), dma((13,)),
            dma((2, 3)), dma((2, 3)),
            dma((2, 4)), dma((2, 4)),
            dma((3,)), dma((3,)),
            dma((2, 8, NP)), dma((2, 8, NP)),
            dma((2, 8, NP)), dma((2, 8, NP)),
            dma((16, NP)), dma((16, NP)),
            dma((3,)), dma((3,)), dma((3,)), dma((3,)), dma((3,)), dma((3,)),
        ],
        compiler_params=pltpu.CompilerParams(
            collective_id=0, has_side_effects=True, vmem_limit_bytes=48 * 2**20
        ),
        name="muon",
    )(momentum)


def solution(mesh):
    return jax.shard_map(
        body, mesh=mesh, in_specs=(P("row", "col"),), out_specs=P("row", "col"), check_vma=False
    )
```

```python
import functools
import math

import jax
import jax.numpy as jnp
from jax import lax
from jax.experimental import pallas as pl
from jax.experimental.pallas import tpu as pltpu
from jax.sharding import PartitionSpec as P

ROWS = 4608
COLS = 8192

quintic_a = 3.4445
quintic_b = -4.775
quintic_c = 2.0315

MESH = pl.DeviceIdType.MESH
F32 = jnp.float32
BF16 = jnp.bfloat16

BLOCK = 288
WIDTH = 256
PANEL = 4 * BLOCK
HALF = PANEL // 2
GROUP = 384
GROUPS = PANEL // GROUP
CHUNK = 112
STACK = 16 * CHUNK
PARTS = ((0, 32), (32, 32), (64, 32), (96, 16))
NP = len(PARTS)
SIDE = WIDTH // 2
STEP4 = (1, 3, 2)


def rows_product(left, right):
    return lax.dot_general(left, right, (((1,), (1,)), ((), ())), preferred_element_type=F32)


def columns_product(left, right):
    return lax.dot_general(left, right, (((0,), (0,)), ((), ())), preferred_element_type=F32)


def kernel(
    m_ref,
    out_ref,
    m_b, row_b, col_b, row_ob, col_ob, x_f, x_b,
    part, gram, ring_p, ring_m,
    tiles, tile_in,
    w, wb, wb2, y_all, y_in, z_in, y_own,
    tile_s, tile_r, bulk_s, bulk_r, pass_s, pass_r, wide_s, wide_r,
    rs_s, rs_r, ag_s, ag_r, swap_s, swap_r,
    ys_s, ys_r, yg_s, yg_r, zs_s, zs_r,
):
    row, col = lax.axis_index("row"), lax.axis_index("col")
    y, x, z, k = row // 4, row % 4, col // 2, col % 2
    first = k == 0

    def at_x(d):
        return (y * 4 + (x + d) % 4, col)

    def at_y(d):
        return (((y + d) % 4) * 4 + x, col)

    def at_z(d):
        return (row, ((z + d) % 16) * 2 + k)

    other = (row, z * 2 + 1 - k)

    o_sum, o_all = jnp.where(first, x, y), jnp.where(first, y, x)

    def ring_sum(d):
        t = (o_sum + d) % 4
        return t, (jnp.where(first, y * 4 + t, t * 4 + x), col)

    def ring_all(d):
        t = (o_all + d) % 4
        return (jnp.where(first, t * 4 + x, y * 4 + t), col)

    def send(src, dst, ss, rs, device):
        return pltpu.make_async_remote_copy(
            src_ref=src, dst_ref=dst, send_sem=ss, recv_sem=rs, device_id=device, device_id_type=MESH
        )

    sent = []

    def start(src, dst, ss, rs, device):
        c = send(src, dst, ss, rs, device)
        c.start()
        sent.append(c)
        return c

    barrier = pltpu.get_barrier_semaphore()
    peers = [at_x(d) for d in STEP4] + [at_y(d) for d in STEP4] + [other]
    peers += [at_z(d) for d in (1, 15, 2, 14)]
    for peer in peers:
        pl.semaphore_signal(barrier, inc=1, device_id=peer, device_id_type=MESH)

    def block(ref, t, rows=BLOCK):
        return ref.at[pl.ds(pl.multiple_of(t * rows, 16), rows), :]

    m_b[...] = m_ref[...].astype(BF16)
    squares = m_ref[...] * m_ref[...]
    squares = jnp.sum(squares.reshape(BLOCK // 8, 8, WIDTH), axis=0)
    tiles[0] = squares[:, :128] + squares[:, 128:]

    pl.semaphore_wait(barrier, len(peers))

    bulk = []
    for i, d in enumerate(STEP4):
        bulk.append(start(m_b, block(row_b, x), bulk_s.at[0, i], bulk_r.at[0, i], at_x(d)))
        bulk.append(start(m_b, block(col_b, y), bulk_s.at[1, i], bulk_r.at[1, i], at_y(d)))

    def pass_rows(src, t):
        @pl.when(t // 2 != k)
        def _():
            send(src, block(row_ob, t % 2), pass_s.at[0, t % 2], pass_r.at[0, t % 2], other).start()

    def pass_cols(src, t):
        send(src, block(col_ob, t), pass_s.at[1, t], pass_r.at[1, t], other).start()

    pass_rows(m_b, x)
    pass_cols(m_b, y)

    def exchange(stage, slots):
        for slot, device in slots:
            start(tiles.at[stage], tile_in.at[slot], tile_s.at[slot], tile_r.at[slot], device)

    def gathered(stage, slots):
        total = tiles[stage]
        for slot, device in slots:
            send(tiles.at[0], tile_in.at[slot], tile_s.at[slot], tile_r.at[slot], device).wait_recv()
            total += tile_in[slot]
        tiles[stage + 1] = total

    near = [(0, at_z(1)), (1, at_z(15)), (2, at_z(2))]
    far = [(3, at_z(4)), (4, at_z(12))]
    along_x = [(6 + i, at_x(d)) for i, d in enumerate(STEP4)]
    along_y = [(9 + i, at_y(d)) for i, d in enumerate(STEP4)]
    exchange(0, near)

    block(row_b, x)[...] = m_b[...]
    block(col_b, y)[...] = m_b[...]
    block(x_f, o_all)[...] = m_ref[...]
    part[STACK - 64 : STACK, :] = jnp.zeros((64, GROUP), F32)

    for i, d in enumerate(STEP4):
        bulk[2 * i].wait_recv()
        pass_rows(block(row_b, (x + 4 - d) % 4), (x + 4 - d) % 4)
        bulk[2 * i + 1].wait_recv()
        pass_cols(block(col_b, (y + 4 - d) % 4), (y + 4 - d) % 4)

    wide = [
        start(m_ref, block(x_f, o_all), wide_s.at[i], wide_r.at[i], ring_all(d)) for i, d in enumerate(STEP4)
    ]

    mine = pl.ds(pl.multiple_of(k * HALF, HALF), HALF)

    def gram_own(n, carry):
        at = pl.ds(pl.multiple_of(n * GROUP, GROUP), GROUP)
        part[pl.ds(pl.multiple_of(n * HALF, HALF), HALF), :] = rows_product(row_b[mine, :], col_b[at, :])
        return carry

    lax.fori_loop(0, GROUPS, gram_own, 0)
    for t in range(2):
        send(m_b, block(row_ob, t), pass_s.at[0, t], pass_r.at[0, t], other).wait_recv()
    for t in range(4):
        send(m_b, block(col_ob, t), pass_s.at[1, t], pass_r.at[1, t], other).wait_recv()

    def gram_other(n, carry):
        at = pl.ds(pl.multiple_of(n * GROUP, GROUP), GROUP)
        part[pl.ds(pl.multiple_of(n * HALF, HALF), HALF), :] += rows_product(row_ob[...], col_ob[at, :])
        return carry

    lax.fori_loop(0, GROUPS, gram_other, 0)

    def piece(c, p):
        return pl.ds(pl.multiple_of((c + 32) % 16 * CHUNK + PARTS[p][0], 16), PARTS[p][1])

    def inside(p):
        return pl.ds(PARTS[p][0], PARTS[p][1])

    def hop(d, s, p):
        ring = (ring_p, ring_m)[d]
        return send(
            ring.at[s, inside(p)], ring.at[s + 1, inside(p)],
            rs_s.at[d, s, p], rs_r.at[d, s, p], (at_z(1), at_z(15))[d],
        )

    def jump(p):
        return send(
            ring_p.at[0, inside(p)], ring_p.at[9, inside(p)], rs_s.at[0, 0, p], rs_r.at[0, 0, p], at_z(2)
        )

    for p in range(NP):
        ring_p[0, inside(p)] = part[piece(z + 8, p), :].astype(BF16)
        jump(p).start()
        ring_m[0, inside(p)] = part[piece(z - 7, p), :].astype(BF16)
        hop(1, 0, p).start()
    for p in range(NP):
        ring_p[1, inside(p)] = part[piece(z + 7, p), :].astype(BF16)
        hop(0, 1, p).start()

    def plus_step(s, p):
        hop(0, s - 1, p).wait_recv()
        ring_p[s, inside(p)] = (ring_p[s, inside(p)].astype(F32) + part[piece(z + 8 - s, p), :]).astype(BF16)
        hop(0, s, p).start()

    def minus_step(s, p):
        hop(1, s - 1, p).wait_recv()
        ring_m[s, inside(p)] = (ring_m[s, inside(p)].astype(F32) + part[piece(z - 7 + s, p), :]).astype(BF16)
        hop(1, s, p).start()

    def reduce_step(s, carry):
        for p in range(NP):
            plus_step(s, p)
            minus_step(s, p)
        return carry

    gathered(0, near)
    for p in range(NP):
        minus_step(1, p)
    for p in range(NP):
        jump(p).wait_recv()
        hop(0, 1, p).wait_recv()
        total = ring_p[2, inside(p)].astype(F32) + ring_p[9, inside(p)].astype(F32) + part[piece(z + 6, p), :]
        ring_p[2, inside(p)] = total.astype(BF16)
        hop(0, 2, p).start()
        minus_step(2, p)
    lax.fori_loop(3, 4, reduce_step, 0)
    exchange(1, far)
    lax.fori_loop(4, 6, reduce_step, 0)
    send(tiles.at[1], tile_in.at[3], tile_s.at[3], tile_r.at[3], at_z(4)).wait_recv()
    onward_tile = start(tile_in.at[3], tile_in.at[5], tile_s.at[5], tile_r.at[5], at_z(4))
    lax.fori_loop(6, 7, reduce_step, 0)
    for p in range(NP):
        plus_step(7, p)
    send(tiles.at[1], tile_in.at[4], tile_s.at[4], tile_r.at[4], at_z(12)).wait_recv()
    onward_tile.wait_recv()
    tiles[2] = tiles[1] + tile_in[3] + tile_in[4] + tile_in[5]
    exchange(2, along_x)

    def onward(d, s, p):
        at = gram.at[k, piece((z - s, z + s)[d], p)]
        return send(at, at, ag_s.at[d, s, p], ag_r.at[d, s, p], (at_z(1), at_z(15))[d])

    def arrived(d, s, p):
        at = gram.at[k, piece((z - s, z + s)[d], p)]
        send(at, at, ag_s.at[d, s - 1, p], ag_r.at[d, s - 1, p], (at_z(1), at_z(15))[d]).wait_recv()

    def chunk(c):
        return pl.ds(pl.multiple_of((c + 32) % 16 * CHUNK, 16), CHUNK)

    def swap(slot, c):
        at = gram.at[k, chunk(c)]
        return send(at, at, swap_s.at[slot], swap_r.at[slot], other)

    def swapped(slot):
        at = gram.at[1 - k, 0:CHUNK]
        send(at, at, swap_s.at[slot], swap_r.at[slot], other).wait_recv()

    for p in range(NP):
        hop(0, 7, p).wait_recv()
        hop(1, 6, p).wait_recv()
        total = part[piece(z, p), :] + ring_p[8, inside(p)].astype(F32) + ring_m[7, inside(p)].astype(F32)
        gram[k, piece(z, p), :] = total.astype(BF16)
        onward(0, 0, p).start()
        onward(1, 0, p).start()
    swap(0, z).start()

    def gather_step(s, carry):
        for p in range(NP):
            arrived(0, s, p)
            onward(0, s, p).start()
            arrived(1, s, p)
            onward(1, s, p).start()
        swap(s, z - s).start()
        swap(8 + s, z + s).start()
        return carry

    lax.fori_loop(1, 3, gather_step, 0)
    gathered(2, along_x)
    exchange(3, along_y)
    lax.fori_loop(3, 5, gather_step, 0)
    gathered(3, along_y)
    exchange(4, [(12, other)])
    lax.fori_loop(5, 6, gather_step, 0)
    gathered(4, [(12, other)])
    norm_squares = jnp.sum(tiles[5])
    factor = 0.6 * math.sqrt(ROWS) / (jnp.sqrt(jnp.full((8, 128), norm_squares, F32)) + 1e-07)
    factor = factor[0:1, 0:1]
    for p in range(NP):
        arrived(0, 6, p)
        at = gram.at[k, piece(z - 6, p)]
        send(at, at, ag_s.at[0, 7, p], ag_r.at[0, 7, p], at_z(2)).start()
        onward(0, 6, p).start()
        arrived(1, 6, p)
        onward(1, 6, p).start()
    swap(6, z - 6).start()
    swap(14, z + 6).start()

    for c in wide:
        c.wait_recv()

    def scale(t, carry):
        at = pl.ds(pl.multiple_of(t * BLOCK, 16), BLOCK)
        rounded = (x_f[at, :] * factor).astype(BF16)
        x_b[0, at, :] = rounded[:, :SIDE]
        x_b[1, at, :] = rounded[:, SIDE:]
        return carry

    lax.fori_loop(0, 4, scale, 0)

    for p in range(NP):
        arrived(0, 7, p)
        arrived(1, 7, p)
    swap(7, z - 7).start()
    swap(15, z + 7).start()
    for slot in (0, 1, 2, 3, 4, 5, 6, 9, 10, 11, 12, 13, 14):
        swapped(slot)
    for p in range(NP):
        arrived(0, 8, p)
    swap(8, z - 8).start()
    for slot in (7, 15, 8):
        swapped(slot)

    squared_factor = factor * factor

    def times_gram(panel, keep, c):
        @pl.when(first)
        def _():
            def half(h, carry):
                total = jnp.zeros((HALF, SIDE), F32)
                for n in range(GROUPS):
                    total += jnp.dot(
                        gram[h, n * HALF : (n + 1) * HALF, :],
                        panel[c, n * GROUP : (n + 1) * GROUP, :],
                        preferred_element_type=F32,
                    )
                at = pl.ds(pl.multiple_of(h * HALF, HALF), HALF)
                total = total * squared_factor
                w[c, at, :] = total
                keep[c, at, :] = total.astype(BF16)
                return carry

            lax.fori_loop(0, 2, half, 0)

        @pl.when(k == 1)
        def _():
            def group(n, carry):
                total = jnp.zeros((GROUP, SIDE), F32)
                for h in range(2):
                    total += columns_product(
                        gram[h, pl.ds(pl.multiple_of(n * HALF, HALF), HALF), :],
                        panel[c, h * HALF : (h + 1) * HALF, :],
                    )
                at = pl.ds(pl.multiple_of(n * GROUP, GROUP), GROUP)
                total = total * squared_factor
                w[c, at, :] = total
                keep[c, at, :] = total.astype(BF16)
                return carry

            lax.fori_loop(0, GROUPS, group, 0)

    def side(ref, c, t):
        return ref.at[c, pl.ds(pl.multiple_of(t * BLOCK, 16), BLOCK), :]

    def scatter(src, dst, ss, rs, c):
        copies = []
        for i, d in enumerate(STEP4):
            t, device = ring_sum(d)
            copies.append(send(side(src, c, t), dst.at[c, i], ss.at[c, i], rs.at[c, i], device))
            copies[-1].start()
        return copies

    def summed(copies, dst, c):
        total = side(w, c, o_sum)[...]
        for i, copy in enumerate(copies):
            copy.wait_recv()
            total += dst[c, i].astype(F32)
        return total

    y_sum = []
    for c in range(2):
        times_gram(x_b, wb, c)
        y_sum.append(scatter(wb, y_in, ys_s, ys_r, c))

    def left(s, carry):
        for p in range(NP):
            hop(0, s, p).wait_send()
            hop(1, s, p).wait_send()
        return carry

    lax.fori_loop(0, 7, left, 0)
    for p in range(NP):
        hop(0, 7, p).wait_send()

    y_gather = []
    for c in range(2):
        total = summed(y_sum[c], y_in, c)
        y_own[c] = total
        side(y_all, c, o_all)[...] = total.astype(BF16)
        copies = []
        for i, d in enumerate(STEP4):
            copies.append(
                send(side(y_all, c, o_all), side(y_all, c, o_all), yg_s.at[c, i], yg_r.at[c, i], ring_all(d))
            )
            copies[-1].start()
        y_gather.append(copies)

    def left_too(s, carry):
        for p in range(NP):
            onward(0, s, p).wait_send()
            onward(1, s, p).wait_send()
        return carry

    lax.fori_loop(0, 7, left_too, 0)
    for p in range(NP):
        onward(0, 7, p).wait_send()

    z_sum = []
    for c in range(2):
        for copy in y_gather[c]:
            copy.wait_recv()
        times_gram(y_all, wb2, c)
        z_sum.append(scatter(wb2, z_in, zs_s, zs_r, c))

    for c in sent:
        c.wait_send()
    for t in range(2):
        send(block(row_ob, t), block(row_ob, t), pass_s.at[0, t], pass_r.at[0, t], other).wait_send()
    for t in range(4):
        send(block(col_ob, t), block(col_ob, t), pass_s.at[1, t], pass_r.at[1, t], other).wait_send()
    for slot in range(16):
        swap(slot, z).wait_send()
    for copies in y_sum + y_gather:
        for copy in copies:
            copy.wait_send()

    for c in range(2):
        z_own = summed(z_sum[c], z_in, c)
        scaled = side(x_b, c, o_all)[...].astype(F32)
        total = quintic_b * y_own[c] + quintic_c * z_own
        out_ref[:, c * SIDE : (c + 1) * SIDE] = math.sqrt(COLS) * (quintic_a * scaled + total)
    for copies in z_sum:
        for copy in copies:
            copy.wait_send()


def body(momentum):
    dma = pltpu.SemaphoreType.DMA
    return pl.pallas_call(
        kernel,
        out_shape=jax.ShapeDtypeStruct((BLOCK, WIDTH), F32),
        in_specs=[pl.BlockSpec(memory_space=pltpu.VMEM)],
        out_specs=pl.BlockSpec(memory_space=pltpu.VMEM),
        scratch_shapes=[
            pltpu.VMEM((BLOCK, WIDTH), BF16),
            pltpu.VMEM((PANEL, WIDTH), BF16),
            pltpu.VMEM((PANEL, WIDTH), BF16),
            pltpu.VMEM((HALF, WIDTH), BF16),
            pltpu.VMEM((PANEL, WIDTH), BF16),
            pltpu.VMEM((PANEL, WIDTH), F32),
            pltpu.VMEM((2, PANEL, SIDE), BF16),
            pltpu.VMEM((STACK, GROUP), F32),
            pltpu.VMEM((2, STACK, GROUP), BF16),
            pltpu.VMEM((10, CHUNK, GROUP), BF16),
            pltpu.VMEM((8, CHUNK, GROUP), BF16),
            pltpu.VMEM((6, 8, 128), F32),
            pltpu.VMEM((13, 8, 128), F32),
            pltpu.VMEM((2, PANEL, SIDE), F32),
            pltpu.VMEM((2, PANEL, SIDE), BF16),
            pltpu.VMEM((2, PANEL, SIDE), BF16),
            pltpu.VMEM((2, PANEL, SIDE), BF16),
            pltpu.VMEM((2, 3, BLOCK, SIDE), BF16),
            pltpu.VMEM((2, 3, BLOCK, SIDE), BF16),
            pltpu.VMEM((2, BLOCK, SIDE), F32),
            dma((13,)), dma((13,)),
            dma((2, 3)), dma((2, 3)),
            dma((2, 4)), dma((2, 4)),
            dma((3,)), dma((3,)),
            dma((2, 8, NP)), dma((2, 8, NP)),
            dma((2, 8, NP)), dma((2, 8, NP)),
            dma((16,)), dma((16,)),
            dma((2, 3)), dma((2, 3)), dma((2, 3)), dma((2, 3)), dma((2, 3)), dma((2, 3)),
        ],
        compiler_params=pltpu.CompilerParams(
            collective_id=0, has_side_effects=True, vmem_limit_bytes=48 * 2**20
        ),
        name="muon",
    )(momentum)


def solution(mesh):
    return jax.shard_map(
        body, mesh=mesh, in_specs=(P("row", "col"),), out_specs=P("row", "col"), check_vma=False
    )
```

```python
import functools
import math

import jax
import jax.numpy as jnp
from jax import lax
from jax.experimental import pallas as pl
from jax.experimental.pallas import tpu as pltpu
from jax.sharding import PartitionSpec as P

ROWS = 4608
COLS = 8192

quintic_a = 3.4445
quintic_b = -4.775
quintic_c = 2.0315

MESH = pl.DeviceIdType.MESH
F32 = jnp.float32
BF16 = jnp.bfloat16

BLOCK = 288
WIDTH = 256
SHARE = BLOCK // 2
PANEL = 4 * BLOCK
HALF = PANEL // 2
GROUP = 384
GROUPS = PANEL // GROUP
CHUNK = 112
STACK = 16 * CHUNK
PARTS = ((0, 32), (32, 32), (64, 32), (96, 16))
NP = len(PARTS)
SIDE = WIDTH // 2
STEP4 = (1, 3, 2)


def rows_product(left, right):
    return lax.dot_general(left, right, (((1,), (1,)), ((), ())), preferred_element_type=F32)


def columns_product(left, right):
    return lax.dot_general(left, right, (((0,), (0,)), ((), ())), preferred_element_type=F32)


def kernel(
    m_ref,
    out_ref,
    m_b, row_b, col_b, row_ob, col_ob, x_f, x_b,
    part, gram, ring_p, ring_m,
    tiles, tile_in,
    w, wb, wb2, y_all, y_in, z_in, y_own,
    tile_s, tile_r, bulk_s, bulk_r, pass_s, pass_r, wide_s, wide_r,
    rs_s, rs_r, ag_s, ag_r, swap_s, swap_r,
    ys_s, ys_r, yg_s, yg_r, zs_s, zs_r,
):
    row, col = lax.axis_index("row"), lax.axis_index("col")
    y, x, z, k = lax.div(row, 4), lax.rem(row, 4), lax.div(col, 2), lax.rem(col, 2)
    first = k == 0

    def at_x(d):
        return (y * 4 + lax.rem(x + d, 4), col)

    def at_y(d):
        return (lax.rem(y + d, 4) * 4 + x, col)

    def at_z(d):
        return (row, lax.rem(z + d, 16) * 2 + k)

    other = (row, z * 2 + 1 - k)
    ways, two_on = (at_z(1), at_z(15)), at_z(2)

    o_sum, o_all = jnp.where(first, x, y), jnp.where(first, y, x)

    def ring_sum(d):
        t = lax.rem(o_sum + d, 4)
        return t, (jnp.where(first, y * 4 + t, t * 4 + x), col)

    def ring_all(d):
        t = lax.rem(o_all + d, 4)
        return (jnp.where(first, t * 4 + x, y * 4 + t), col)

    def send(src, dst, ss, rs, device):
        return pltpu.make_async_remote_copy(
            src_ref=src, dst_ref=dst, send_sem=ss, recv_sem=rs, device_id=device, device_id_type=MESH
        )

    sent = []

    def start(src, dst, ss, rs, device):
        c = send(src, dst, ss, rs, device)
        c.start()
        sent.append(c)
        return c

    barrier = pltpu.get_barrier_semaphore()
    peers = [at_x(1), at_x(3), at_y(1), at_y(3), at_z(1), at_z(15), other]
    for peer in peers:
        pl.semaphore_signal(barrier, inc=1, device_id=peer, device_id_type=MESH)

    def block(ref, t, rows=BLOCK):
        return ref.at[pl.ds(pl.multiple_of(t * rows, 16), rows), :]

    m_b[...] = m_ref[...].astype(BF16)
    squares = m_ref[...] * m_ref[...]
    squares = jnp.sum(squares.reshape(BLOCK // 8, 8, WIDTH), axis=0)
    tiles[0] = squares[:, :128] + squares[:, 128:]

    pl.semaphore_wait(barrier, len(peers))

    def half_of(ref, t, h):
        return ref.at[pl.ds(pl.multiple_of(t * BLOCK + h * SHARE, 16), SHARE), :]

    rings = ((row_b, x, at_x(1), at_x(3)), (col_b, y, at_y(1), at_y(3)))

    def bulk(j, way, step, onward=False):
        panel, here, after, before = rings[j]
        h = (way + step) % 2
        t = here
        if onward:
            t = lax.rem(here + (3, 1)[way], 4)
        src = half_of(panel, t, h) if onward else half_of(m_b, 0, h)
        return send(
            src, half_of(panel, t, h), bulk_s.at[j, way, step], bulk_r.at[j, way, step], (after, before)[way]
        )

    def came(j, way, step):
        here = rings[j][1]
        return lax.rem(here + ((3, 3, 2), (1, 1, 2))[way][step], 4), (way + step) % 2

    for step in range(2):
        for way in range(2):
            for j in range(2):
                sent.append(bulk(j, way, step))
                sent[-1].start()

    def pass_rows(src, t, h):
        slot = lax.rem(t, 2) * 2 + h

        @pl.when(lax.div(t, 2) != k)
        def _():
            send(src, half_of(row_ob, lax.rem(t, 2), h), pass_s.at[0, slot], pass_r.at[0, slot], other).start()

    def pass_cols(src, t, h):
        slot = t * 2 + h
        send(src, half_of(col_ob, t, h), pass_s.at[1, slot], pass_r.at[1, slot], other).start()

    def passed(j, slot):
        ref = (row_ob, col_ob)[j]
        at = ref.at[slot * SHARE : (slot + 1) * SHARE, :]
        return send(at, at, pass_s.at[j, slot], pass_r.at[j, slot], other)

    def pass_on(j, t, h):
        (pass_rows, pass_cols)[j](half_of(rings[j][0], t, h), t, h)

    for h in range(2):
        pass_rows(half_of(m_b, 0, h), x, h)
        pass_cols(half_of(m_b, 0, h), y, h)

    def exchange(stage, slots):
        for slot, device in slots:
            start(tiles.at[stage], tile_in.at[slot], tile_s.at[slot], tile_r.at[slot], device)

    def gathered(stage, slots):
        total = tiles[stage]
        for slot, device in slots:
            send(tiles.at[0], tile_in.at[slot], tile_s.at[slot], tile_r.at[slot], device).wait_recv()
            total += tile_in[slot]
        tiles[stage + 1] = total

    near = [(0, at_z(1)), (1, at_z(15)), (2, at_z(2))]
    far = [(3, at_z(4)), (4, at_z(12))]
    along_x = [(6 + i, at_x(d)) for i, d in enumerate(STEP4)]
    along_y = [(9 + i, at_y(d)) for i, d in enumerate(STEP4)]
    exchange(0, near[:2])

    block(row_b, x)[...] = m_b[...]
    block(col_b, y)[...] = m_b[...]
    block(x_f, o_all)[...] = m_ref[...]
    part[STACK - 64 : STACK, :] = jnp.zeros((64, GROUP), F32)

    for way in range(2):
        for j in range(2):
            bulk(j, way, 0).wait_recv()
            sent.append(bulk(j, way, 2, True))
            sent[-1].start()
            pass_on(j, *came(j, way, 0))
    for step in (1, 2):
        for way in range(2):
            for j in range(2):
                bulk(j, way, step).wait_recv()
                pass_on(j, *came(j, way, step))

    for slot, device in near[:2]:
        send(tiles.at[0], tile_in.at[slot], tile_s.at[slot], tile_r.at[slot], device).wait_recv()
    exchange(0, near[2:])

    wide = [
        start(m_ref, block(x_f, o_all), wide_s.at[i], wide_r.at[i], ring_all(d)) for i, d in enumerate(STEP4)
    ]

    mine = pl.ds(pl.multiple_of(k * HALF, HALF), HALF)

    def gram_own(n, carry):
        at = pl.ds(pl.multiple_of(n * GROUP, GROUP), GROUP)
        part[pl.ds(pl.multiple_of(n * HALF, HALF), HALF), :] = rows_product(row_b[mine, :], col_b[at, :])
        return carry

    lax.fori_loop(0, GROUPS, gram_own, 0)
    for slot in range(4):
        passed(0, slot).wait_recv()
    for slot in range(8):
        passed(1, slot).wait_recv()

    def gram_other(n, carry):
        at = pl.ds(pl.multiple_of(n * GROUP, GROUP), GROUP)
        part[pl.ds(pl.multiple_of(n * HALF, HALF), HALF), :] += rows_product(row_ob[...], col_ob[at, :])
        return carry

    lax.fori_loop(0, GROUPS, gram_other, 0)

    def piece(c, p):
        return pl.ds(pl.multiple_of(lax.rem(c + 32, 16) * CHUNK + PARTS[p][0], 16), PARTS[p][1])

    def inside(p):
        return pl.ds(PARTS[p][0], PARTS[p][1])

    def hop(d, s, p):
        ring = (ring_p, ring_m)[d]
        return send(
            ring.at[s, inside(p)], ring.at[s + 1, inside(p)],
            rs_s.at[d, s, p], rs_r.at[d, s, p], ways[d],
        )

    def jump(p):
        return send(
            ring_p.at[0, inside(p)], ring_p.at[9, inside(p)], rs_s.at[0, 0, p], rs_r.at[0, 0, p], two_on
        )

    for p in range(NP):
        ring_p[0, inside(p)] = part[piece(z + 8, p), :].astype(BF16)
        jump(p).start()
        ring_m[0, inside(p)] = part[piece(z - 7, p), :].astype(BF16)
        hop(1, 0, p).start()
    for p in range(NP):
        ring_p[1, inside(p)] = part[piece(z + 7, p), :].astype(BF16)
        hop(0, 1, p).start()

    def plus_step(s, p):
        hop(0, s - 1, p).wait_recv()
        ring_p[s, inside(p)] = (ring_p[s, inside(p)].astype(F32) + part[piece(z + 8 - s, p), :]).astype(BF16)
        hop(0, s, p).start()

    def minus_step(s, p):
        hop(1, s - 1, p).wait_recv()
        ring_m[s, inside(p)] = (ring_m[s, inside(p)].astype(F32) + part[piece(z - 7 + s, p), :]).astype(BF16)
        hop(1, s, p).start()

    def reduce_step(s, carry):
        for p in range(NP):
            plus_step(s, p)
            minus_step(s, p)
        return carry

    for p in range(NP):
        minus_step(1, p)
    for p in range(NP):
        jump(p).wait_recv()
        hop(0, 1, p).wait_recv()
        total = ring_p[2, inside(p)].astype(F32) + ring_p[9, inside(p)].astype(F32) + part[piece(z + 6, p), :]
        ring_p[2, inside(p)] = total.astype(BF16)
        hop(0, 2, p).start()
        minus_step(2, p)
    send(tiles.at[0], tile_in.at[2], tile_s.at[2], tile_r.at[2], two_on).wait_recv()
    tiles[1] = tiles[0] + tile_in[0] + tile_in[1] + tile_in[2]
    lax.fori_loop(3, 4, reduce_step, 0)
    exchange(1, far)
    lax.fori_loop(4, 6, reduce_step, 0)
    send(tiles.at[1], tile_in.at[3], tile_s.at[3], tile_r.at[3], at_z(4)).wait_recv()
    onward_tile = start(tile_in.at[3], tile_in.at[5], tile_s.at[5], tile_r.at[5], at_z(4))
    lax.fori_loop(6, 7, reduce_step, 0)
    for p in range(NP):
        plus_step(7, p)
    send(tiles.at[1], tile_in.at[4], tile_s.at[4], tile_r.at[4], at_z(12)).wait_recv()
    onward_tile.wait_recv()
    tiles[2] = tiles[1] + tile_in[3] + tile_in[4] + tile_in[5]
    exchange(2, along_x)

    def onward(d, s, p):
        at = gram.at[k, piece((z - s, z + s)[d], p)]
        return send(at, at, ag_s.at[d, s, p], ag_r.at[d, s, p], ways[d])

    def arrived(d, s, p):
        at = gram.at[k, piece((z - s, z + s)[d], p)]
        send(at, at, ag_s.at[d, s - 1, p], ag_r.at[d, s - 1, p], ways[d]).wait_recv()

    def chunk(c):
        return pl.ds(pl.multiple_of(lax.rem(c + 32, 16) * CHUNK, 16), CHUNK)

    def swap(slot, c):
        at = gram.at[k, chunk(c)]
        return send(at, at, swap_s.at[slot], swap_r.at[slot], other)

    def swapped(slot):
        at = gram.at[1 - k, 0:CHUNK]
        send(at, at, swap_s.at[slot], swap_r.at[slot], other).wait_recv()

    for p in range(NP):
        hop(0, 7, p).wait_recv()
        hop(1, 6, p).wait_recv()
        total = part[piece(z, p), :] + ring_p[8, inside(p)].astype(F32) + ring_m[7, inside(p)].astype(F32)
        gram[k, piece(z, p), :] = total.astype(BF16)
        onward(0, 0, p).start()
        onward(1, 0, p).start()
    swap(0, z).start()

    def gather_step(s, carry):
        for p in range(NP):
            arrived(0, s, p)
            onward(0, s, p).start()
            arrived(1, s, p)
            onward(1, s, p).start()
        swap(s, z - s).start()
        swap(8 + s, z + s).start()
        return carry

    lax.fori_loop(1, 3, gather_step, 0)
    gathered(2, along_x)
    exchange(3, along_y)
    lax.fori_loop(3, 5, gather_step, 0)
    gathered(3, along_y)
    exchange(4, [(12, other)])
    lax.fori_loop(5, 6, gather_step, 0)
    gathered(4, [(12, other)])
    norm_squares = jnp.sum(tiles[5])
    factor = 0.6 * math.sqrt(ROWS) / (jnp.sqrt(jnp.full((8, 128), norm_squares, F32)) + 1e-07)
    factor = factor[0:1, 0:1]
    for p in range(NP):
        arrived(0, 6, p)
        at = gram.at[k, piece(z - 6, p)]
        send(at, at, ag_s.at[0, 7, p], ag_r.at[0, 7, p], two_on).start()
        onward(0, 6, p).start()
        arrived(1, 6, p)
        onward(1, 6, p).start()
    swap(6, z - 6).start()
    swap(14, z + 6).start()

    for c in wide:
        c.wait_recv()

    def scale(t, carry):
        at = pl.ds(pl.multiple_of(t * BLOCK, 16), BLOCK)
        rounded = (x_f[at, :] * factor).astype(BF16)
        x_b[0, at, :] = rounded[:, :SIDE]
        x_b[1, at, :] = rounded[:, SIDE:]
        return carry

    lax.fori_loop(0, 4, scale, 0)

    for p in range(NP):
        arrived(0, 7, p)
        arrived(1, 7, p)
    swap(7, z - 7).start()
    swap(15, z + 7).start()
    for slot in (0, 1, 2, 3, 4, 5, 6, 9, 10, 11, 12, 13, 14):
        swapped(slot)
    for p in range(NP):
        arrived(0, 8, p)
    swap(8, z - 8).start()
    for slot in (7, 15, 8):
        swapped(slot)

    squared_factor = factor * factor

    def times_gram(panel, keep, c):
        @pl.when(first)
        def _():
            def half(h, carry):
                total = jnp.zeros((HALF, SIDE), F32)
                for n in range(GROUPS):
                    total += jnp.dot(
                        gram[h, n * HALF : (n + 1) * HALF, :],
                        panel[c, n * GROUP : (n + 1) * GROUP, :],
                        preferred_element_type=F32,
                    )
                at = pl.ds(pl.multiple_of(h * HALF, HALF), HALF)
                total = total * squared_factor
                w[c, at, :] = total
                keep[c, at, :] = total.astype(BF16)
                return carry

            lax.fori_loop(0, 2, half, 0)

        @pl.when(k == 1)
        def _():
            def group(n, carry):
                total = jnp.zeros((GROUP, SIDE), F32)
                for h in range(2):
                    total += columns_product(
                        gram[h, pl.ds(pl.multiple_of(n * HALF, HALF), HALF), :],
                        panel[c, h * HALF : (h + 1) * HALF, :],
                    )
                at = pl.ds(pl.multiple_of(n * GROUP, GROUP), GROUP)
                total = total * squared_factor
                w[c, at, :] = total
                keep[c, at, :] = total.astype(BF16)
                return carry

            lax.fori_loop(0, GROUPS, group, 0)

    def side(ref, c, t):
        return ref.at[c, pl.ds(pl.multiple_of(t * BLOCK, 16), BLOCK), :]

    def scatter(src, dst, ss, rs, c):
        copies = []
        for i, d in enumerate(STEP4):
            t, device = ring_sum(d)
            copies.append(send(side(src, c, t), dst.at[c, i], ss.at[c, i], rs.at[c, i], device))
            copies[-1].start()
        return copies

    def summed(copies, dst, c):
        total = side(w, c, o_sum)[...]
        for i, copy in enumerate(copies):
            copy.wait_recv()
            total += dst[c, i].astype(F32)
        return total

    y_sum = []
    for c in range(2):
        times_gram(x_b, wb, c)
        y_sum.append(scatter(wb, y_in, ys_s, ys_r, c))

    def left(s, carry):
        for p in range(NP):
            hop(0, s, p).wait_send()
            hop(1, s, p).wait_send()
        return carry

    lax.fori_loop(0, 7, left, 0)
    for p in range(NP):
        hop(0, 7, p).wait_send()

    y_gather = []
    for c in range(2):
        total = summed(y_sum[c], y_in, c)
        y_own[c] = total
        side(y_all, c, o_all)[...] = total.astype(BF16)
        copies = []
        for i, d in enumerate(STEP4):
            copies.append(
                send(side(y_all, c, o_all), side(y_all, c, o_all), yg_s.at[c, i], yg_r.at[c, i], ring_all(d))
            )
            copies[-1].start()
        y_gather.append(copies)

    def left_too(s, carry):
        for p in range(NP):
            onward(0, s, p).wait_send()
            onward(1, s, p).wait_send()
        return carry

    lax.fori_loop(0, 7, left_too, 0)
    for p in range(NP):
        onward(0, 7, p).wait_send()

    z_sum = []
    for c in range(2):
        for copy in y_gather[c]:
            copy.wait_recv()
        times_gram(y_all, wb2, c)
        z_sum.append(scatter(wb2, z_in, zs_s, zs_r, c))

    for c in sent:
        c.wait_send()
    for slot in range(4):
        passed(0, slot).wait_send()
    for slot in range(8):
        passed(1, slot).wait_send()
    for slot in range(16):
        swap(slot, z).wait_send()
    for copies in y_sum + y_gather:
        for copy in copies:
            copy.wait_send()

    for c in range(2):
        z_own = summed(z_sum[c], z_in, c)
        scaled = side(x_b, c, o_all)[...].astype(F32)
        total = quintic_b * y_own[c] + quintic_c * z_own
        out_ref[:, c * SIDE : (c + 1) * SIDE] = math.sqrt(COLS) * (quintic_a * scaled + total)
    for copies in z_sum:
        for copy in copies:
            copy.wait_send()


def body(momentum):
    dma = pltpu.SemaphoreType.DMA
    return pl.pallas_call(
        kernel,
        out_shape=jax.ShapeDtypeStruct((BLOCK, WIDTH), F32),
        in_specs=[pl.BlockSpec(memory_space=pltpu.VMEM)],
        out_specs=pl.BlockSpec(memory_space=pltpu.VMEM),
        scratch_shapes=[
            pltpu.VMEM((BLOCK, WIDTH), BF16),
            pltpu.VMEM((PANEL, WIDTH), BF16),
            pltpu.VMEM((PANEL, WIDTH), BF16),
            pltpu.VMEM((HALF, WIDTH), BF16),
            pltpu.VMEM((PANEL, WIDTH), BF16),
            pltpu.VMEM((PANEL, WIDTH), F32),
            pltpu.VMEM((2, PANEL, SIDE), BF16),
            pltpu.VMEM((STACK, GROUP), F32),
            pltpu.VMEM((2, STACK, GROUP), BF16),
            pltpu.VMEM((10, CHUNK, GROUP), BF16),
            pltpu.VMEM((8, CHUNK, GROUP), BF16),
            pltpu.VMEM((6, 8, 128), F32),
            pltpu.VMEM((13, 8, 128), F32),
            pltpu.VMEM((2, PANEL, SIDE), F32),
            pltpu.VMEM((2, PANEL, SIDE), BF16),
            pltpu.VMEM((2, PANEL, SIDE), BF16),
            pltpu.VMEM((2, PANEL, SIDE), BF16),
            pltpu.VMEM((2, 3, BLOCK, SIDE), BF16),
            pltpu.VMEM((2, 3, BLOCK, SIDE), BF16),
            pltpu.VMEM((2, BLOCK, SIDE), F32),
            dma((13,)), dma((13,)),
            dma((2, 2, 3)), dma((2, 2, 3)),
            dma((2, 8)), dma((2, 8)),
            dma((3,)), dma((3,)),
            dma((2, 8, NP)), dma((2, 8, NP)),
            dma((2, 8, NP)), dma((2, 8, NP)),
            dma((16,)), dma((16,)),
            dma((2, 3)), dma((2, 3)), dma((2, 3)), dma((2, 3)), dma((2, 3)), dma((2, 3)),
        ],
        compiler_params=pltpu.CompilerParams(
            collective_id=0, has_side_effects=True, vmem_limit_bytes=48 * 2**20
        ),
        name="muon",
    )(momentum)


def solution(mesh):
    return jax.shard_map(
        body, mesh=mesh, in_specs=(P("row", "col"),), out_specs=P("row", "col"), check_vma=False
    )
```

```python
import functools
import math

import jax
import jax.numpy as jnp
from jax import lax
from jax.experimental import pallas as pl
from jax.experimental.pallas import tpu as pltpu
from jax.sharding import PartitionSpec as P

ROWS = 4608
COLS = 8192

quintic_a = 3.4445
quintic_b = -4.775
quintic_c = 2.0315

MESH = pl.DeviceIdType.MESH
F32 = jnp.float32
BF16 = jnp.bfloat16

BLOCK = 288
WIDTH = 256
SHARE = BLOCK // 2
PANEL = 4 * BLOCK
HALF = PANEL // 2
GROUP = 384
GROUPS = PANEL // GROUP
CHUNK = 112
STACK = 16 * CHUNK
PARTS = ((0, 32), (32, 32), (64, 32), (96, 16))
NP = len(PARTS)
SIDE = WIDTH // 2
STEP4 = (1, 3, 2)


def rows_product(left, right):
    return lax.dot_general(left, right, (((1,), (1,)), ((), ())), preferred_element_type=F32)


def columns_product(left, right):
    return lax.dot_general(left, right, (((0,), (0,)), ((), ())), preferred_element_type=F32)


def kernel(
    m_ref,
    out_ref,
    m_b, row_b, col_b, row_ob, col_ob, x_f, x_b,
    part, gram, ring_p, ring_m,
    tiles, tile_in,
    w, wb, wb2, y_all, y_in, z_in, y_own,
    tile_s, tile_r, bulk_s, bulk_r, pass_s, pass_r, wide_s, wide_r,
    rs_s, rs_r, ag_s, ag_r, swap_s, swap_r,
    ys_s, ys_r, yg_s, yg_r, zs_s, zs_r,
):
    row, col = lax.axis_index("row"), lax.axis_index("col")
    y, x, z, k = lax.div(row, 4), lax.rem(row, 4), lax.div(col, 2), lax.rem(col, 2)
    first = k == 0

    def at_x(d):
        return (y * 4 + lax.rem(x + d, 4), col)

    def at_y(d):
        return (lax.rem(y + d, 4) * 4 + x, col)

    def at_z(d):
        return (row, lax.rem(z + d, 16) * 2 + k)

    other = (row, z * 2 + 1 - k)
    ways, two_on, two_back = (at_z(1), at_z(15)), at_z(2), at_z(14)

    o_sum, o_all = jnp.where(first, x, y), jnp.where(first, y, x)

    def ring_sum(d):
        t = lax.rem(o_sum + d, 4)
        return t, (jnp.where(first, y * 4 + t, t * 4 + x), col)

    def ring_all(d):
        t = lax.rem(o_all + d, 4)
        return (jnp.where(first, t * 4 + x, y * 4 + t), col)

    def send(src, dst, ss, rs, device):
        return pltpu.make_async_remote_copy(
            src_ref=src, dst_ref=dst, send_sem=ss, recv_sem=rs, device_id=device, device_id_type=MESH
        )

    sent = []

    def start(src, dst, ss, rs, device):
        c = send(src, dst, ss, rs, device)
        c.start()
        sent.append(c)
        return c

    barrier = pltpu.get_barrier_semaphore()
    peers = [at_x(1), at_x(3), at_y(1), at_y(3), at_z(1), at_z(15), other]
    for peer in peers:
        pl.semaphore_signal(barrier, inc=1, device_id=peer, device_id_type=MESH)

    def block(ref, t, rows=BLOCK):
        return ref.at[pl.ds(pl.multiple_of(t * rows, 16), rows), :]

    m_b[...] = m_ref[...].astype(BF16)
    squares = m_ref[...] * m_ref[...]
    squares = jnp.sum(squares.reshape(BLOCK // 8, 8, WIDTH), axis=0)
    tiles[0] = squares[:, :128] + squares[:, 128:]

    pl.semaphore_wait(barrier, len(peers))

    def half_of(ref, t, h):
        return ref.at[pl.ds(pl.multiple_of(t * BLOCK + h * SHARE, 16), SHARE), :]

    rings = ((row_b, x, at_x(1), at_x(3)), (col_b, y, at_y(1), at_y(3)))

    def bulk(j, way, step, onward=False):
        panel, here, after, before = rings[j]
        h = (way + step) % 2
        t = here
        if onward:
            t = lax.rem(here + (3, 1)[way], 4)
        src = half_of(panel, t, h) if onward else half_of(m_b, 0, h)
        return send(
            src, half_of(panel, t, h), bulk_s.at[j, way, step], bulk_r.at[j, way, step], (after, before)[way]
        )

    def came(j, way, step):
        here = rings[j][1]
        return lax.rem(here + ((3, 3, 2), (1, 1, 2))[way][step], 4), (way + step) % 2

    for step in range(2):
        for way in range(2):
            for j in range(2):
                sent.append(bulk(j, way, step))
                sent[-1].start()

    def pass_rows(src, t, h):
        slot = lax.rem(t, 2) * 2 + h

        @pl.when(lax.div(t, 2) != k)
        def _():
            send(src, half_of(row_ob, lax.rem(t, 2), h), pass_s.at[0, slot], pass_r.at[0, slot], other).start()

    def pass_cols(src, t, h):
        slot = t * 2 + h
        send(src, half_of(col_ob, t, h), pass_s.at[1, slot], pass_r.at[1, slot], other).start()

    def passed(j, slot):
        ref = (row_ob, col_ob)[j]
        at = ref.at[slot * SHARE : (slot + 1) * SHARE, :]
        return send(at, at, pass_s.at[j, slot], pass_r.at[j, slot], other)

    def pass_on(j, t, h):
        (pass_rows, pass_cols)[j](half_of(rings[j][0], t, h), t, h)

    for h in range(2):
        pass_rows(half_of(m_b, 0, h), x, h)
        pass_cols(half_of(m_b, 0, h), y, h)

    def exchange(stage, slots):
        for slot, device in slots:
            start(tiles.at[stage], tile_in.at[slot], tile_s.at[slot], tile_r.at[slot], device)

    def gathered(stage, slots):
        total = tiles[stage]
        for slot, device in slots:
            send(tiles.at[0], tile_in.at[slot], tile_s.at[slot], tile_r.at[slot], device).wait_recv()
            total += tile_in[slot]
        tiles[stage + 1] = total

    near = [(0, at_z(1)), (1, at_z(15)), (2, at_z(2))]
    far = [(3, at_z(4)), (4, at_z(12))]
    along_x = [(6 + i, at_x(d)) for i, d in enumerate(STEP4)]
    along_y = [(9 + i, at_y(d)) for i, d in enumerate(STEP4)]
    exchange(0, near[:2])

    block(row_b, x)[...] = m_b[...]
    block(col_b, y)[...] = m_b[...]
    block(x_f, o_all)[...] = m_ref[...]
    part[STACK - 64 : STACK, :] = jnp.zeros((64, GROUP), F32)

    for way in range(2):
        for j in range(2):
            bulk(j, way, 0).wait_recv()
            sent.append(bulk(j, way, 2, True))
            sent[-1].start()
            pass_on(j, *came(j, way, 0))
    for step in (1, 2):
        for way in range(2):
            for j in range(2):
                bulk(j, way, step).wait_recv()
                pass_on(j, *came(j, way, step))

    for slot, device in near[:2]:
        send(tiles.at[0], tile_in.at[slot], tile_s.at[slot], tile_r.at[slot], device).wait_recv()
    exchange(0, near[2:])

    wide = [
        start(m_ref, block(x_f, o_all), wide_s.at[i], wide_r.at[i], ring_all(d)) for i, d in enumerate(STEP4)
    ]

    mine = pl.ds(pl.multiple_of(k * HALF, HALF), HALF)

    def gram_own(n, carry):
        at = pl.ds(pl.multiple_of(n * GROUP, GROUP), GROUP)
        part[pl.ds(pl.multiple_of(n * HALF, HALF), HALF), :] = rows_product(row_b[mine, :], col_b[at, :])
        return carry

    lax.fori_loop(0, GROUPS, gram_own, 0)
    for slot in range(4):
        passed(0, slot).wait_recv()
    for slot in range(8):
        passed(1, slot).wait_recv()

    def gram_other(n, carry):
        at = pl.ds(pl.multiple_of(n * GROUP, GROUP), GROUP)
        part[pl.ds(pl.multiple_of(n * HALF, HALF), HALF), :] += rows_product(row_ob[...], col_ob[at, :])
        return carry

    lax.fori_loop(0, GROUPS, gram_other, 0)

    def piece(c, p):
        return pl.ds(pl.multiple_of(lax.rem(c + 32, 16) * CHUNK + PARTS[p][0], 16), PARTS[p][1])

    def inside(p):
        return pl.ds(PARTS[p][0], PARTS[p][1])

    def hop(d, s, p):
        ring = (ring_p, ring_m)[d]
        return send(
            ring.at[s, inside(p)], ring.at[s + 1, inside(p)],
            rs_s.at[d, s, p], rs_r.at[d, s, p], ways[d],
        )

    for p in range(NP):
        ring_p[0, inside(p)] = part[piece(z + 8, p), :].astype(BF16)
        hop(0, 0, p).start()
        ring_m[0, inside(p)] = part[piece(z - 7, p), :].astype(BF16)
        hop(1, 0, p).start()

    def plus_step(s, p):
        hop(0, s - 1, p).wait_recv()
        ring_p[s, inside(p)] = (ring_p[s, inside(p)].astype(F32) + part[piece(z + 8 - s, p), :]).astype(BF16)
        hop(0, s, p).start()

    def minus_step(s, p):
        hop(1, s - 1, p).wait_recv()
        ring_m[s, inside(p)] = (ring_m[s, inside(p)].astype(F32) + part[piece(z - 7 + s, p), :]).astype(BF16)
        hop(1, s, p).start()

    def reduce_step(s, carry):
        for p in range(NP):
            plus_step(s, p)
            minus_step(s, p)
        return carry

    lax.fori_loop(1, 3, reduce_step, 0)
    send(tiles.at[0], tile_in.at[2], tile_s.at[2], tile_r.at[2], two_on).wait_recv()
    tiles[1] = tiles[0] + tile_in[0] + tile_in[1] + tile_in[2]
    lax.fori_loop(3, 4, reduce_step, 0)
    exchange(1, far)
    lax.fori_loop(4, 6, reduce_step, 0)
    send(tiles.at[1], tile_in.at[3], tile_s.at[3], tile_r.at[3], at_z(4)).wait_recv()
    onward_tile = start(tile_in.at[3], tile_in.at[5], tile_s.at[5], tile_r.at[5], at_z(4))
    lax.fori_loop(6, 7, reduce_step, 0)
    for p in range(NP):
        plus_step(7, p)
    send(tiles.at[1], tile_in.at[4], tile_s.at[4], tile_r.at[4], at_z(12)).wait_recv()
    onward_tile.wait_recv()
    tiles[2] = tiles[1] + tile_in[3] + tile_in[4] + tile_in[5]
    exchange(2, along_x)

    def onward(d, s, p):
        at = gram.at[k, piece((z - s, z + s)[d], p)]
        return send(at, at, ag_s.at[d, s, p], ag_r.at[d, s, p], ways[d])

    def arrived(d, s, p):
        at = gram.at[k, piece((z - s, z + s)[d], p)]
        send(at, at, ag_s.at[d, s - 1, p], ag_r.at[d, s - 1, p], ways[d]).wait_recv()

    def chunk(c):
        return pl.ds(pl.multiple_of(lax.rem(c + 32, 16) * CHUNK, 16), CHUNK)

    def swap(slot, c):
        at = gram.at[k, chunk(c)]
        return send(at, at, swap_s.at[slot], swap_r.at[slot], other)

    def swapped(slot):
        at = gram.at[1 - k, 0:CHUNK]
        send(at, at, swap_s.at[slot], swap_r.at[slot], other).wait_recv()

    for p in range(NP):
        hop(0, 7, p).wait_recv()
        hop(1, 6, p).wait_recv()
        total = part[piece(z, p), :] + ring_p[8, inside(p)].astype(F32) + ring_m[7, inside(p)].astype(F32)
        gram[k, piece(z, p), :] = total.astype(BF16)
        onward(0, 0, p).start()
        onward(1, 0, p).start()
    swap(0, z).start()

    def gather_step(s, carry):
        for p in range(NP):
            arrived(0, s, p)
            onward(0, s, p).start()
            arrived(1, s, p)
            onward(1, s, p).start()
        swap(s, z - s).start()
        swap(8 + s, z + s).start()
        return carry

    lax.fori_loop(1, 3, gather_step, 0)
    gathered(2, along_x)
    exchange(3, along_y)
    def leap(d, s, p):
        at = gram.at[k, piece((z - s, z + s)[d], p)]
        return send(at, at, ag_s.at[d, s + 1, p], ag_r.at[d, s + 1, p], (two_on, two_back)[d])

    lax.fori_loop(3, 4, gather_step, 0)
    for p in range(NP):
        arrived(0, 4, p)
        leap(0, 4, p).start()
        onward(0, 4, p).start()
        arrived(1, 4, p)
        onward(1, 4, p).start()
    swap(4, z - 4).start()
    swap(12, z + 4).start()
    gathered(3, along_y)
    exchange(4, [(12, other)])
    for p in range(NP):
        arrived(1, 5, p)
        leap(1, 5, p).start()
        onward(1, 5, p).start()
        arrived(0, 5, p)
    swap(5, z - 5).start()
    swap(13, z + 5).start()
    gathered(4, [(12, other)])
    norm_squares = jnp.sum(tiles[5])
    factor = 0.6 * math.sqrt(ROWS) / (jnp.sqrt(jnp.full((8, 128), norm_squares, F32)) + 1e-07)
    factor = factor[0:1, 0:1]
    for p in range(NP):
        arrived(0, 6, p)
        leap(0, 6, p).start()
        onward(0, 6, p).start()
        arrived(1, 6, p)
    swap(6, z - 6).start()
    swap(14, z + 6).start()

    for c in wide:
        c.wait_recv()

    def scale(t, carry):
        at = pl.ds(pl.multiple_of(t * BLOCK, 16), BLOCK)
        rounded = (x_f[at, :] * factor).astype(BF16)
        x_b[0, at, :] = rounded[:, :SIDE]
        x_b[1, at, :] = rounded[:, SIDE:]
        return carry

    lax.fori_loop(0, 4, scale, 0)

    for p in range(NP):
        arrived(0, 7, p)
        arrived(1, 7, p)
    swap(7, z - 7).start()
    swap(15, z + 7).start()
    for slot in (0, 1, 2, 3, 4, 5, 6, 9, 10, 11, 12, 13, 14):
        swapped(slot)
    for p in range(NP):
        arrived(0, 8, p)
    swap(8, z - 8).start()
    for slot in (7, 15, 8):
        swapped(slot)

    squared_factor = factor * factor

    def times_gram(panel, keep, c):
        @pl.when(first)
        def _():
            def half(h, carry):
                total = jnp.zeros((HALF, SIDE), F32)
                for n in range(GROUPS):
                    total += jnp.dot(
                        gram[h, n * HALF : (n + 1) * HALF, :],
                        panel[c, n * GROUP : (n + 1) * GROUP, :],
                        preferred_element_type=F32,
                    )
                at = pl.ds(pl.multiple_of(h * HALF, HALF), HALF)
                total = total * squared_factor
                w[c, at, :] = total
                keep[c, at, :] = total.astype(BF16)
                return carry

            lax.fori_loop(0, 2, half, 0)

        @pl.when(k == 1)
        def _():
            def group(n, carry):
                total = jnp.zeros((GROUP, SIDE), F32)
                for h in range(2):
                    total += columns_product(
                        gram[h, pl.ds(pl.multiple_of(n * HALF, HALF), HALF), :],
                        panel[c, h * HALF : (h + 1) * HALF, :],
                    )
                at = pl.ds(pl.multiple_of(n * GROUP, GROUP), GROUP)
                total = total * squared_factor
                w[c, at, :] = total
                keep[c, at, :] = total.astype(BF16)
                return carry

            lax.fori_loop(0, GROUPS, group, 0)

    def side(ref, c, t):
        return ref.at[c, pl.ds(pl.multiple_of(t * BLOCK, 16), BLOCK), :]

    def scatter(src, dst, ss, rs, c):
        copies = []
        for i, d in enumerate(STEP4):
            t, device = ring_sum(d)
            copies.append(send(side(src, c, t), dst.at[c, i], ss.at[c, i], rs.at[c, i], device))
            copies[-1].start()
        return copies

    def summed(copies, dst, c):
        total = side(w, c, o_sum)[...]
        for i, copy in enumerate(copies):
            copy.wait_recv()
            total += dst[c, i].astype(F32)
        return total

    y_sum = []
    for c in range(2):
        times_gram(x_b, wb, c)
        y_sum.append(scatter(wb, y_in, ys_s, ys_r, c))

    def left(s, carry):
        for p in range(NP):
            hop(0, s, p).wait_send()
            hop(1, s, p).wait_send()
        return carry

    lax.fori_loop(0, 7, left, 0)
    for p in range(NP):
        hop(0, 7, p).wait_send()

    y_gather = []
    for c in range(2):
        total = summed(y_sum[c], y_in, c)
        y_own[c] = total
        side(y_all, c, o_all)[...] = total.astype(BF16)
        copies = []
        for i, d in enumerate(STEP4):
            copies.append(
                send(side(y_all, c, o_all), side(y_all, c, o_all), yg_s.at[c, i], yg_r.at[c, i], ring_all(d))
            )
            copies[-1].start()
        y_gather.append(copies)

    def left_too(s, carry):
        for p in range(NP):
            onward(0, s, p).wait_send()
            onward(1, s, p).wait_send()
        return carry

    lax.fori_loop(0, 7, left_too, 0)
    for p in range(NP):
        onward(0, 7, p).wait_send()

    z_sum = []
    for c in range(2):
        for copy in y_gather[c]:
            copy.wait_recv()
        times_gram(y_all, wb2, c)
        z_sum.append(scatter(wb2, z_in, zs_s, zs_r, c))

    for c in sent:
        c.wait_send()
    for slot in range(4):
        passed(0, slot).wait_send()
    for slot in range(8):
        passed(1, slot).wait_send()
    for slot in range(16):
        swap(slot, z).wait_send()
    for copies in y_sum + y_gather:
        for copy in copies:
            copy.wait_send()

    for c in range(2):
        z_own = summed(z_sum[c], z_in, c)
        scaled = side(x_b, c, o_all)[...].astype(F32)
        total = quintic_b * y_own[c] + quintic_c * z_own
        out_ref[:, c * SIDE : (c + 1) * SIDE] = math.sqrt(COLS) * (quintic_a * scaled + total)
    for copies in z_sum:
        for copy in copies:
            copy.wait_send()


def body(momentum):
    dma = pltpu.SemaphoreType.DMA
    return pl.pallas_call(
        kernel,
        out_shape=jax.ShapeDtypeStruct((BLOCK, WIDTH), F32),
        in_specs=[pl.BlockSpec(memory_space=pltpu.VMEM)],
        out_specs=pl.BlockSpec(memory_space=pltpu.VMEM),
        scratch_shapes=[
            pltpu.VMEM((BLOCK, WIDTH), BF16),
            pltpu.VMEM((PANEL, WIDTH), BF16),
            pltpu.VMEM((PANEL, WIDTH), BF16),
            pltpu.VMEM((HALF, WIDTH), BF16),
            pltpu.VMEM((PANEL, WIDTH), BF16),
            pltpu.VMEM((PANEL, WIDTH), F32),
            pltpu.VMEM((2, PANEL, SIDE), BF16),
            pltpu.VMEM((STACK, GROUP), F32),
            pltpu.VMEM((2, STACK, GROUP), BF16),
            pltpu.VMEM((10, CHUNK, GROUP), BF16),
            pltpu.VMEM((8, CHUNK, GROUP), BF16),
            pltpu.VMEM((6, 8, 128), F32),
            pltpu.VMEM((13, 8, 128), F32),
            pltpu.VMEM((2, PANEL, SIDE), F32),
            pltpu.VMEM((2, PANEL, SIDE), BF16),
            pltpu.VMEM((2, PANEL, SIDE), BF16),
            pltpu.VMEM((2, PANEL, SIDE), BF16),
            pltpu.VMEM((2, 3, BLOCK, SIDE), BF16),
            pltpu.VMEM((2, 3, BLOCK, SIDE), BF16),
            pltpu.VMEM((2, BLOCK, SIDE), F32),
            dma((13,)), dma((13,)),
            dma((2, 2, 3)), dma((2, 2, 3)),
            dma((2, 8)), dma((2, 8)),
            dma((3,)), dma((3,)),
            dma((2, 8, NP)), dma((2, 8, NP)),
            dma((2, 8, NP)), dma((2, 8, NP)),
            dma((16,)), dma((16,)),
            dma((2, 3)), dma((2, 3)), dma((2, 3)), dma((2, 3)), dma((2, 3)), dma((2, 3)),
        ],
        compiler_params=pltpu.CompilerParams(
            collective_id=0, has_side_effects=True, vmem_limit_bytes=48 * 2**20
        ),
        name="muon",
    )(momentum)


def solution(mesh):
    return jax.shard_map(
        body, mesh=mesh, in_specs=(P("row", "col"),), out_specs=P("row", "col"), check_vma=False
    )
```
